32 devices in a mesh: seq: 4 (over x, core), head: 2 (over y), dp: 4 (over z).
Axes of the slice: x: 2, y: 2, z: 4, core: 2. Of those that a mesh axis runs over, the one named last changes fastest.
Arguments:
- queries: bfloat16 [8192, 4096], P(('dp', 'seq'), 'head'), parts along dimension 0, may hold values from -6 to 6
- key_vectors: bfloat16 [8192, 4096], P(('dp', 'seq'), 'head'), parts along dimension 0, may hold values from -6 to 6
- value_vectors: bfloat16 [8192, 4096], P(('dp', 'seq'), 'head'), parts along dimension 0, may hold values from -13 to 13
- norm_gain: float32 [4096], P('head'), may hold values from 0.1 to 1.9
- cotangent: bfloat16 [8192, 4096], P(('dp', 'seq'), 'head'), parts along dimension 0, may hold values from -6 to 6
Outputs:
- layer_out: bfloat16 [8192, 4096], P(('dp', 'seq'), 'head'), parts along dimension 0
- grad_query: bfloat16 [8192, 4096], P(('dp', 'seq'), 'head'), parts along dimension 0
- grad_key: bfloat16 [8192, 4096], P(('dp', 'seq'), 'head'), parts along dimension 0
- grad_value: bfloat16 [8192, 4096], P(('dp', 'seq'), 'head'), parts along dimension 0
The draws below stay inside these ranges and needn't reach their ends.
There are 4 independent parts, one for each index of `dp`. The reference program is written for one: setup_inputs(seed, part) draws one part's arguments, and reference() takes and returns one part's arrays. A program takes and returns all parts, laid end to end along the dimension named above; an argument that names none is the same for every part. Nothing has to cross between parts.
All inputs are finite; a program needn't handle non-finite values.
Results may differ from the reference program's by a relative error of at most 0.0058.
Values sent between devices are 32-bit elements; how exact they have to be, the bound alone decides.
A program may use at most 64 MiB of HBM per device.

```python
import jax
import jax.numpy as jnp
from jax import lax

HD = 128
HEADS = 32
BLOCK = 512
TOKENS = 2048
FEAT = 4096


def draw_value_vectors(key, part):
    key = jax.random.fold_in(key, 11)
    subkeys = jax.random.split(key, 3)
    row_scale = 10.0 ** (0.5 * jax.random.uniform(subkeys[0], (TOKENS, 1)))
    position = (jnp.arange(HEADS * HD) // HD).astype(jnp.float32) / max(HEADS - 1, 1)
    spread = jax.random.uniform(subkeys[1], (HEADS * HD,))
    col_scale = 10.0 ** (0.5 * position + 0.5 * spread)
    noise = jnp.clip(jax.random.normal(subkeys[2], (TOKENS, HEADS * HD)), -4.0, 4.0)
    return (0.1 * noise * row_scale * col_scale).astype(jnp.bfloat16)


def block_levels(rng, extent, cuts, smallest, high):
    factor_of, own = 1.0, jax.random.fold_in(rng, 6)
    for axis_at, parts in cuts:
        draws = jnp.exp(jax.random.uniform(jax.random.fold_in(own, axis_at), (parts,), jnp.float32, smallest / len(cuts), high / len(cuts)))
        factor_of = factor_of * jnp.repeat(draws, extent[axis_at] // parts).reshape([-1 if axis == axis_at else 1 for axis in range(len(extent))])
    return factor_of


def bell_draw(stream_key, extent, scale, limit, pieces=(), held_as=jnp.bfloat16):
    array = scale * jax.random.normal(stream_key, extent, jnp.float32)
    if pieces:
        array = array * block_levels(stream_key, extent, pieces, -0.22, 0.18)
    return jnp.clip(array, -limit, limit).astype(held_as)


def setup_inputs(seed: int = 0, part: int = 0) -> dict:
    key_list = jax.random.split(jax.random.key(seed), 6)
    part_keys = jax.random.split(jax.random.fold_in(key_list[5], part), 6)
    return {
        "queries": bell_draw(part_keys[0], (TOKENS, FEAT), 1.0, 6.0, ((0, 4), (1, 2))),
        "key_vectors": bell_draw(part_keys[1], (TOKENS, FEAT), 1.0, 6.0, ((0, 4), (1, 2))),
        "value_vectors": draw_value_vectors(jax.random.fold_in(jax.random.fold_in(key_list[5], part), 71), part),
        "norm_gain": jnp.clip(1.0 + 0.18 * jax.random.normal(key_list[3], (FEAT,), jnp.float32), 0.1, 1.9),
        "cotangent": bell_draw(part_keys[4], (TOKENS, FEAT), 1.0, 6.0, ((0, 4), (1, 2))),
    }


EPS = 1e-06

def to_low(values_in):
    return lax.optimization_barrier(values_in.astype(jnp.bfloat16)).astype(jnp.float32)

def reference(queries, key_vectors, value_vectors, norm_gain, cotangent):
    highest = lax.Precision.HIGHEST
    block_count = TOKENS // BLOCK
    block_shape = (block_count, BLOCK, HEADS, HD)
    query_blocks = queries.astype(jnp.float32).reshape(block_shape)
    key_blocks = key_vectors.astype(jnp.float32).reshape(block_shape)
    value_blocks = value_vectors.astype(jnp.float32).reshape(block_shape)
    positions = jnp.arange(BLOCK)
    causal = positions[:, None] >= positions[None, :]

    def forward_step(prefix_state, blocks):
        query_b, key_b, value_b = blocks
        prefix_low = to_low(prefix_state)
        scores = jnp.einsum('thd,shd->hts', query_b, key_b, precision=highest)
        block_weights = to_low(jnp.where(causal, scores, 0.0))
        attended = jnp.einsum('thd,hde->the', query_b, prefix_low, precision=highest)
        attended = attended + jnp.einsum('hts,she->the', block_weights, value_b, precision=highest)
        local_kv = jnp.einsum('shd,she->hde', key_b, value_b, precision=highest)
        return (prefix_state + local_kv, (attended, prefix_state))
    start_state = jnp.zeros((HEADS, HD, HD), jnp.float32)
    _, (attended_blocks, prefix_states) = lax.scan(forward_step, start_state, (query_blocks, key_blocks, value_blocks))
    attended = attended_blocks.reshape(TOKENS, FEAT)
    inverse_rms = lax.rsqrt(lax.optimization_barrier(jnp.sum(attended * attended, axis=1)) / FEAT + EPS)[:, None]
    layer_out = (attended * inverse_rms * norm_gain).astype(jnp.bfloat16)
    scaled_grad = cotangent.astype(jnp.float32) * norm_gain
    inner = lax.optimization_barrier(jnp.sum(scaled_grad * attended, axis=1))[:, None]
    out_grad = to_low(inverse_rms * (scaled_grad - attended * inner * inverse_rms * inverse_rms / FEAT))
    grad_blocks = out_grad.reshape(block_shape)

    def backward_step(suffix_state, blocks):
        query_b, key_b, value_b, grad_b, prefix_state = blocks
        suffix_low = to_low(suffix_state)
        prefix_low = to_low(prefix_state)
        scores = jnp.einsum('thd,shd->hts', query_b, key_b, precision=highest)
        block_weights = to_low(jnp.where(causal, scores, 0.0))
        grad_scores = jnp.einsum('the,she->hts', grad_b, value_b, precision=highest)
        grad_weights = to_low(jnp.where(causal, grad_scores, 0.0))
        query_grad = jnp.einsum('the,hde->thd', grad_b, prefix_low, precision=highest)
        query_grad = query_grad + jnp.einsum('hts,shd->thd', grad_weights, key_b, precision=highest)
        key_grad = jnp.einsum('she,hde->shd', value_b, suffix_low, precision=highest)
        key_grad = key_grad + jnp.einsum('hts,thd->shd', grad_weights, query_b, precision=highest)
        value_grad = jnp.einsum('shd,hde->she', key_b, suffix_low, precision=highest)
        value_grad = value_grad + jnp.einsum('hts,the->she', block_weights, grad_b, precision=highest)
        local_qg = jnp.einsum('thd,the->hde', query_b, grad_b, precision=highest)
        return (suffix_state + local_qg, (query_grad, key_grad, value_grad))
    _, (query_grads, key_grads, value_grads) = lax.scan(backward_step, start_state, (query_blocks, key_blocks, value_blocks, grad_blocks, prefix_states), reverse=True)
    grad_query = query_grads.reshape(TOKENS, FEAT).astype(jnp.bfloat16)
    grad_key = key_grads.reshape(TOKENS, FEAT).astype(jnp.bfloat16)
    grad_value = value_grads.reshape(TOKENS, FEAT).astype(jnp.bfloat16)
    return (layer_out, grad_query, grad_key, grad_value)
```

```python
import functools

import jax
import jax.numpy as jnp
from jax import lax
from jax.experimental import pallas as pl
from jax.experimental.pallas import tpu as pltpu
from jax.sharding import PartitionSpec as P

HD = 128
PAIR = 2 * HD
FEAT = 4096
EPS = 1e-06
MESH = pl.DeviceIdType.MESH
F32 = jnp.float32
BF16 = jnp.bfloat16


def dot(a, b, a_dim, b_dim):
    return lax.dot_general(a, b, (((a_dim,), (b_dim,)), ((), ())), preferred_element_type=F32)


def block_diagonal(first, second):
    empty = jnp.zeros_like(first)
    return jnp.concatenate(
        [jnp.concatenate([first, empty], axis=1), jnp.concatenate([empty, second], axis=1)], axis=0
    )


def kernel(
    seq_size, head_size,
    q_hbm, k_hbm, v_hbm, gain_ref, ct_hbm,
    lo_hbm, gq_hbm, gk_hbm, gv_hbm,
    q, k, v, ct, lo, gq, gk, gv,
    weights, att, og, part_k, part_v,
    local, inner_in, total, cross_in, outer, prefix, acc_sq, acc_in, stat_out, stat_in,
    kv_sem, in_sem, out_sem, grad_sem,
    in_send, in_recv, cross_send, cross_recv, fwd_send, fwd_recv, stat_send, stat_recv,
):
    tokens, columns = q.shape
    tile = tokens // 2
    units = columns // PAIR
    half = units // 2
    chips = seq_size // 2
    me = lax.axis_index("seq")
    chip, core = me // 2, me % 2
    head = lax.axis_index("head")
    partner = chip * 2 + 1 - core

    def cols(unit):
        return pl.ds(pl.multiple_of(unit * PAIR, PAIR), PAIR)

    def own_unit(j):
        return core * half + j

    def other_unit(j):
        return (1 - core) * half + j

    def load(i, which):
        unit = lax.rem((1 - core) * half + i, units)
        source, target = ((k_hbm, k), (v_hbm, v))[which]
        return pltpu.make_async_copy(
            source.at[:, cols(unit)], target.at[:, cols(unit)], kv_sem.at[which, i]
        )

    def start_load(i, carry):
        load(i, 0).start()
        load(i, 1).start()
        return carry

    lax.fori_loop(0, units, start_load, 0)
    load_q = pltpu.make_async_copy(q_hbm, q, in_sem.at[0])
    load_ct = pltpu.make_async_copy(ct_hbm, ct, in_sem.at[1])
    load_q.start()
    load_ct.start()

    barrier = pltpu.get_barrier_semaphore()
    pl.semaphore_signal(barrier, inc=1, device_id={"seq": partner}, device_id_type=MESH)
    for d in range(1, chips):
        pl.semaphore_signal(
            barrier, inc=1, device_id={"seq": lax.rem(me + 2 * d, seq_size)}, device_id_type=MESH
        )
    for d in range(1, head_size):
        pl.semaphore_signal(
            barrier, inc=1, device_id={"head": lax.rem(head + d, head_size)}, device_id_type=MESH
        )
    pl.semaphore_wait(barrier, 1 + (chips - 1) + (head_size - 1))

    def states(unit):
        return pl.ds(2 * unit, 2)

    def to_partner(way, i):
        unit = lax.rem((1 - core) * half + i, units)
        return pltpu.make_async_remote_copy(
            src_ref=local.at[way, states(unit)],
            dst_ref=inner_in.at[way, states(unit)],
            send_sem=in_send.at[way, i],
            recv_sem=in_recv.at[way, i],
            device_id={"seq": partner},
            device_id_type=MESH,
        )

    def across(way, d, j):
        step = 2 * d if way == 0 else -2 * d
        return pltpu.make_async_remote_copy(
            src_ref=total.at[way, states(j)],
            dst_ref=cross_in.at[way, d - 1, states(j)],
            send_sem=cross_send.at[way, d - 1, j],
            recv_sem=cross_recv.at[way, d - 1, j],
            device_id={"seq": lax.rem(me + step + seq_size, seq_size)},
            device_id_type=MESH,
        )

    def forward(way, j, unit):
        return pltpu.make_async_remote_copy(
            src_ref=outer.at[way, states(unit)],
            dst_ref=outer.at[way, states(unit)],
            send_sem=fwd_send.at[way, j],
            recv_sem=fwd_recv.at[way, j],
            device_id={"seq": partner},
            device_id_type=MESH,
        )

    def sends_to(way, d):
        return chip + d < chips if way == 0 else chip - d >= 0

    def takes_from(way, d):
        return chip - d >= 0 if way == 0 else chip + d < chips

    def takes_any(way):
        return chip > 0 if way == 0 else chip < chips - 1

    def gives_inner(way):
        return core == 0 if way == 0 else core == 1

    def send_states(way, make):
        def partner_half(i, carry):
            make(i, other_unit(i))
            to_partner(way, i).start()
            return carry

        lax.fori_loop(0, half, partner_half, 0)

        def own_half(j, carry):
            unit = own_unit(j)
            make(half + j, unit)

            @pl.when(gives_inner(way))
            def _():
                to_partner(way, half + j).start()

            to_partner(way, j).wait_recv()
            total[way, states(j)] = local[way, states(unit)] + inner_in[way, states(unit)]
            for d in range(1, chips):

                @pl.when(sends_to(way, d))
                def _():
                    across(way, d, j).start()

            return carry

        lax.fori_loop(0, half, own_half, 0)

    def take_states(way, use):
        def step(j, carry):
            unit = own_unit(j)

            @pl.when(takes_any(way))
            def _():
                outer[way, states(unit)] = jnp.zeros((2, HD, HD), F32)
                for d in range(1, chips):

                    @pl.when(takes_from(way, d))
                    def _():
                        across(way, d, j).wait_recv()
                        outer[way, states(unit)] += cross_in[way, d - 1, states(j)]

                forward(way, j, unit).start()

            @pl.when(jnp.logical_not(takes_any(way)))
            def _():
                outer[way, states(unit)] = jnp.zeros((2, HD, HD), F32)
                outer[way, states(other_unit(j))] = jnp.zeros((2, HD, HD), F32)

            use(unit, low_state(way, unit))

            @pl.when(takes_any(way))
            def _():
                forward(way, j, other_unit(j)).wait_recv()

            @pl.when(jnp.logical_not(gives_inner(way)))
            def _():
                to_partner(way, half + j).wait_recv()

            use(other_unit(j), low_state(way, other_unit(j)))
            return carry

        lax.fori_loop(0, half, step, 0)

    def low_state(way, unit):
        state = outer[way, states(unit)]
        state = jnp.where(gives_inner(way), state, state + inner_in[way, states(unit)])
        state = state.astype(BF16)
        return block_diagonal(state[0], state[1])

    def end_sends(way):
        def step(j, carry):
            to_partner(way, j).wait_send()

            @pl.when(gives_inner(way))
            def _():
                to_partner(way, half + j).wait_send()

            for d in range(1, chips):

                @pl.when(sends_to(way, d))
                def _():
                    across(way, d, j).wait_send()

            @pl.when(takes_any(way))
            def _():
                forward(way, j, own_unit(j)).wait_send()

            return carry

        lax.fori_loop(0, half, step, 0)

    def make_kv(i, unit):
        load(i, 0).wait()
        load(i, 1).wait()
        key, value = k[:, cols(unit)], v[:, cols(unit)]
        for n in range(2):
            at = slice(n * HD, (n + 1) * HD)
            local[0, 2 * unit + n] = dot(key[:, at], value[:, at], 0, 0)

    send_states(0, make_kv)

    causal = lax.broadcasted_iota(jnp.int32, (tile, tile), 0) >= lax.broadcasted_iota(
        jnp.int32, (tile, tile), 1
    )

    def masked(scores):
        return jnp.where(causal, scores, 0.0).astype(BF16)

    acc_sq[...] = jnp.zeros_like(acc_sq)
    acc_in[...] = jnp.zeros_like(acc_in)
    load_q.wait()

    def own_scores(unit, carry):
        query, key, value = q[:, cols(unit)], k[:, cols(unit)], v[:, cols(unit)]
        for n in range(2):
            at = slice(n * HD, (n + 1) * HD)
            qh, kh, vh = query[:, at], key[:, at], value[:, at]
            w00 = masked(dot(qh[:tile], kh[:tile], 1, 1))
            w10 = dot(qh[tile:], kh[:tile], 1, 1).astype(BF16)
            w11 = masked(dot(qh[tile:], kh[tile:], 1, 1))
            weights[2 * unit + n, 0] = w00
            weights[2 * unit + n, 1] = w10
            weights[2 * unit + n, 2] = w11
            where = pl.ds(pl.multiple_of(unit * PAIR + n * HD, HD), HD)
            att[:tile, where] = dot(w00, vh[:tile], 1, 0)
            att[tile:, where] = dot(jnp.concatenate([w10, w11], axis=1), vh, 1, 0)
        return carry

    lax.fori_loop(0, units, own_scores, 0)
    load_ct.wait()

    def add_prefix(unit, low):
        prefix[unit] = low
        attended = att[:, cols(unit)] + dot(q[:, cols(unit)], low, 1, 0)
        att[:, cols(unit)] = attended
        squared = attended * attended
        product = ct[:, cols(unit)].astype(F32) * gain_ref[:, cols(unit)] * attended
        acc_sq[...] += squared[:, :HD] + squared[:, HD:]
        acc_in[...] += product[:, :HD] + product[:, HD:]

    take_states(0, add_prefix)

    stat_out[0:1, :] = jnp.sum(acc_sq[...].T, axis=0, keepdims=True)
    stat_out[1:2, :] = jnp.sum(acc_in[...].T, axis=0, keepdims=True)
    stat_out[2:8, :] = jnp.zeros((6, tokens), F32)

    def stat_copy(d):
        return pltpu.make_async_remote_copy(
            src_ref=stat_out,
            dst_ref=stat_in.at[d - 1],
            send_sem=stat_send.at[d - 1],
            recv_sem=stat_recv.at[d - 1],
            device_id={"head": lax.rem(head + d, head_size)},
            device_id_type=MESH,
        )

    for d in range(1, head_size):
        stat_copy(d).start()
    sums = stat_out[...]
    for d in range(1, head_size):
        stat_copy(d).wait_recv()
        sums = sums + stat_in[d - 1]
    inverse = lax.rsqrt(sums[0:1] / FEAT + EPS)
    scale = sums[1:2] * inverse * inverse * inverse / FEAT
    acc_sq[...] = jnp.broadcast_to(inverse, (HD, tokens)).T
    acc_in[...] = jnp.broadcast_to(scale, (HD, tokens)).T

    def make_qg(i, unit):
        gain = gain_ref[:, cols(unit)]
        inv = jnp.concatenate([acc_sq[...]] * 2, axis=1)
        coef = jnp.concatenate([acc_in[...]] * 2, axis=1)
        attended = att[:, cols(unit)]
        scaled = ct[:, cols(unit)].astype(F32) * gain
        out_grad = (inv * scaled - attended * coef).astype(BF16)
        og[:, cols(unit)] = out_grad
        query = q[:, cols(unit)]
        for n in range(2):
            at = slice(n * HD, (n + 1) * HD)
            local[1, 2 * unit + n] = dot(query[:, at], out_grad[:, at], 0, 0)

    send_states(1, make_qg)

    def finish_forward(unit, carry):
        inv = jnp.concatenate([acc_sq[...]] * 2, axis=1)
        lo[:, cols(unit)] = (att[:, cols(unit)] * inv * gain_ref[:, cols(unit)]).astype(BF16)
        return carry

    lax.fori_loop(0, units, finish_forward, 0)
    write_lo = pltpu.make_async_copy(lo, lo_hbm, out_sem.at[0])
    write_lo.start()

    def own_grads(unit, carry):
        query, key, value = q[:, cols(unit)], k[:, cols(unit)], v[:, cols(unit)]
        grad = og[:, cols(unit)]
        from_prefix = dot(grad, prefix[unit], 1, 1)
        for n in range(2):
            at = slice(n * HD, (n + 1) * HD)
            qh, kh, vh, gh = query[:, at], key[:, at], value[:, at], grad[:, at]
            g00 = masked(dot(gh[:tile], vh[:tile], 1, 1))
            g10 = dot(gh[tile:], vh[:tile], 1, 1).astype(BF16)
            g11 = masked(dot(gh[tile:], vh[tile:], 1, 1))
            w00 = weights[2 * unit + n, 0]
            w10 = weights[2 * unit + n, 1]
            w11 = weights[2 * unit + n, 2]
            where = pl.ds(pl.multiple_of(unit * PAIR + n * HD, HD), HD)
            gq[:tile, where] = (from_prefix[:tile, at] + dot(g00, kh[:tile], 1, 0)).astype(BF16)
            gq[tile:, where] = (
                from_prefix[tile:, at] + dot(jnp.concatenate([g10, g11], axis=1), kh, 1, 0)
            ).astype(BF16)
            part_k[:tile, where] = dot(jnp.concatenate([g00, g10], axis=0), qh, 0, 0)
            part_k[tile:, where] = dot(g11, qh[tile:], 0, 0)
            part_v[:tile, where] = dot(jnp.concatenate([w00, w10], axis=0), gh, 0, 0)
            part_v[tile:, where] = dot(w11, gh[tile:], 0, 0)
        return carry

    lax.fori_loop(0, units, own_grads, 0)
    write_gq = pltpu.make_async_copy(gq, gq_hbm, out_sem.at[1])
    write_gq.start()

    def write_grad(which, unit):
        source, target = ((gk, gk_hbm), (gv, gv_hbm))[which]
        return pltpu.make_async_copy(
            source.at[:, cols(unit)], target.at[:, cols(unit)], grad_sem.at[which, unit]
        )

    def add_suffix(unit, low):
        at = cols(unit)
        gk[:, at] = (part_k[:, at] + dot(v[:, at], low, 1, 1)).astype(BF16)
        write_grad(0, unit).start()
        gv[:, at] = (part_v[:, at] + dot(k[:, at], low, 1, 0)).astype(BF16)
        write_grad(1, unit).start()

    take_states(1, add_suffix)

    def end_writes(unit, carry):
        write_grad(0, unit).wait()
        write_grad(1, unit).wait()
        return carry

    end_sends(0)
    end_sends(1)
    for d in range(1, head_size):
        stat_copy(d).wait_send()
    write_lo.wait()
    write_gq.wait()
    lax.fori_loop(0, units, end_writes, 0)


def per_device(seq_size, head_size, queries, key_vectors, value_vectors, norm_gain, cotangent):
    tokens, columns = queries.shape
    heads = columns // HD
    units = heads // 2
    half = units // 2
    chips = seq_size // 2
    dma = pltpu.SemaphoreType.DMA
    anywhere = pl.BlockSpec(memory_space=pl.ANY)
    narrow = pltpu.VMEM((tokens, columns), BF16)
    wide = pltpu.VMEM((tokens, columns), F32)
    out = jax.ShapeDtypeStruct((tokens, columns), BF16)
    return pl.pallas_call(
        functools.partial(kernel, seq_size, head_size),
        out_shape=(out,) * 4,
        in_specs=[anywhere] * 3 + [pl.BlockSpec(memory_space=pltpu.VMEM), anywhere],
        out_specs=(anywhere,) * 4,
        scratch_shapes=[narrow] * 8
        + [
            pltpu.VMEM((heads, 3, tokens // 2, tokens // 2), BF16),
            wide,
            narrow,
            wide,
            wide,
            pltpu.VMEM((2, heads, HD, HD), F32),
            pltpu.VMEM((2, heads, HD, HD), F32),
            pltpu.VMEM((2, heads // 2, HD, HD), F32),
            pltpu.VMEM((2, max(chips - 1, 1), heads // 2, HD, HD), F32),
            pltpu.VMEM((2, heads, HD, HD), F32),
            pltpu.VMEM((units, PAIR, PAIR), BF16),
            pltpu.VMEM((tokens, HD), F32),
            pltpu.VMEM((tokens, HD), F32),
            pltpu.VMEM((8, tokens), F32),
            pltpu.VMEM((max(head_size - 1, 1), 8, tokens), F32),
            dma((2, units)),
            dma((2,)),
            dma((2,)),
            dma((2, units)),
            dma((2, units)),
            dma((2, units)),
            dma((2, max(chips - 1, 1), half)),
            dma((2, max(chips - 1, 1), half)),
            dma((2, half)),
            dma((2, half)),
            dma((max(head_size - 1, 1),)),
            dma((max(head_size - 1, 1),)),
        ],
        compiler_params=pltpu.CompilerParams(
            collective_id=0, has_side_effects=True, vmem_limit_bytes=60 * 1024 * 1024
        ),
        cost_estimate=pl.CostEstimate(
            flops=12 * tokens * tokens * columns,
            bytes_accessed=16 * tokens * columns,
            transcendentals=tokens,
        ),
    )(queries, key_vectors, value_vectors, norm_gain.reshape(1, columns), cotangent)


def solution(mesh):
    rows, features = P(("dp", "seq"), "head"), P("head")
    return jax.shard_map(
        functools.partial(per_device, mesh.shape["seq"], mesh.shape["head"]),
        mesh=mesh,
        in_specs=(rows, rows, rows, features, rows),
        out_specs=(rows,) * 4,
        check_vma=False,
    )
```

```python
import functools

import jax
import jax.numpy as jnp
from jax import lax
from jax.experimental import pallas as pl
from jax.experimental.pallas import tpu as pltpu
from jax.sharding import PartitionSpec as P

HD = 128
PAIR = 2 * HD
FEAT = 4096
EPS = 1e-06
MESH = pl.DeviceIdType.MESH
F32 = jnp.float32
BF16 = jnp.bfloat16


def dot(a, b, a_dim, b_dim):
    return lax.dot_general(a, b, (((a_dim,), (b_dim,)), ((), ())), preferred_element_type=F32)


def block_diagonal(first, second):
    empty = jnp.zeros_like(first)
    return jnp.concatenate(
        [jnp.concatenate([first, empty], axis=1), jnp.concatenate([empty, second], axis=1)], axis=0
    )


def kernel(
    seq_size, head_size,
    q_hbm, k_hbm, v_hbm, gain_ref, ct_hbm,
    lo, gq, gk, gv,
    q, k, v, ct,
    weights, att, og, part_v,
    local, inner_in, total, cross_in, outer, prefix, acc_sq, acc_in, stat_out, stat_in,
    kv_sem, in_sem,
    in_send, in_recv, cross_send, cross_recv, fwd_send, fwd_recv, stat_send, stat_recv,
):
    tokens, columns = q.shape
    tile = tokens // 2
    units = columns // PAIR
    half = units // 2
    chips = seq_size // 2
    me = lax.axis_index("seq")
    chip, core = me // 2, me % 2
    head = lax.axis_index("head")
    partner = chip * 2 + 1 - core

    def cols(unit):
        return pl.ds(pl.multiple_of(unit * PAIR, PAIR), PAIR)

    def own_unit(j):
        return core * half + j

    def other_unit(j):
        return (1 - core) * half + j

    def load(i, which):
        unit = lax.rem((1 - core) * half + i, units)
        source, target = ((k_hbm, k), (v_hbm, v))[which]
        return pltpu.make_async_copy(
            source.at[:, cols(unit)], target.at[:, cols(unit)], kv_sem.at[which, i]
        )

    def start_load(i, carry):
        for n in (i, half + i):
            load(n, 0).start()
            load(n, 1).start()
        return carry

    lax.fori_loop(0, half, start_load, 0)
    load_q = pltpu.make_async_copy(q_hbm, q, in_sem.at[0])
    load_ct = pltpu.make_async_copy(ct_hbm, ct, in_sem.at[1])

    barrier = pltpu.get_barrier_semaphore()
    pl.semaphore_signal(barrier, inc=1, device_id={"seq": partner}, device_id_type=MESH)
    for d in range(1, chips):
        pl.semaphore_signal(
            barrier, inc=1, device_id={"seq": lax.rem(me + 2 * d, seq_size)}, device_id_type=MESH
        )
    for d in range(1, head_size):
        pl.semaphore_signal(
            barrier, inc=1, device_id={"head": lax.rem(head + d, head_size)}, device_id_type=MESH
        )
    pl.semaphore_wait(barrier, 1 + (chips - 1) + (head_size - 1))

    def states(unit):
        return pl.ds(2 * unit, 2)

    def to_partner(way, i):
        unit = lax.rem((1 - core) * half + i, units)
        return pltpu.make_async_remote_copy(
            src_ref=local.at[way, states(unit)],
            dst_ref=inner_in.at[way, states(unit)],
            send_sem=in_send.at[way, i],
            recv_sem=in_recv.at[way, i],
            device_id={"seq": partner},
            device_id_type=MESH,
        )

    def across(way, d, j):
        step = 2 * d if way == 0 else -2 * d
        return pltpu.make_async_remote_copy(
            src_ref=total.at[way, states(j)],
            dst_ref=cross_in.at[way, d - 1, states(j)],
            send_sem=cross_send.at[way, d - 1, j],
            recv_sem=cross_recv.at[way, d - 1, j],
            device_id={"seq": lax.rem(me + step + seq_size, seq_size)},
            device_id_type=MESH,
        )

    def forward(way, j, unit):
        return pltpu.make_async_remote_copy(
            src_ref=outer.at[way, states(unit)],
            dst_ref=outer.at[way, states(unit)],
            send_sem=fwd_send.at[way, j],
            recv_sem=fwd_recv.at[way, j],
            device_id={"seq": partner},
            device_id_type=MESH,
        )

    def sends_to(way, d):
        return chip + d < chips if way == 0 else chip - d >= 0

    def takes_from(way, d):
        return chip - d >= 0 if way == 0 else chip + d < chips

    def takes_any(way):
        return chip > 0 if way == 0 else chip < chips - 1

    def gives_inner(way):
        return core == 0 if way == 0 else core == 1

    def send_states(way, make):
        def give_other(i):
            make(i, other_unit(i))
            to_partner(way, i).start()

        give_other(0)

        def step(j, carry):
            unit = own_unit(j)
            make(half + j, unit)

            @pl.when(gives_inner(way))
            def _():
                to_partner(way, half + j).start()

            @pl.when(j + 1 < half)
            def _():
                give_other(j + 1)

            to_partner(way, j).wait_recv()
            total[way, states(j)] = local[way, states(unit)] + inner_in[way, states(unit)]
            for d in range(1, chips):

                @pl.when(sends_to(way, d))
                def _():
                    across(way, d, j).start()

            return carry

        lax.fori_loop(0, half, step, 0)

    def take_states(way, use):
        def step(j, carry):
            unit = own_unit(j)

            @pl.when(takes_any(way))
            def _():
                outer[way, states(unit)] = jnp.zeros((2, HD, HD), F32)
                for d in range(1, chips):

                    @pl.when(takes_from(way, d))
                    def _():
                        across(way, d, j).wait_recv()
                        outer[way, states(unit)] += cross_in[way, d - 1, states(j)]

                forward(way, j, unit).start()

            @pl.when(jnp.logical_not(takes_any(way)))
            def _():
                outer[way, states(unit)] = jnp.zeros((2, HD, HD), F32)
                outer[way, states(other_unit(j))] = jnp.zeros((2, HD, HD), F32)

            use(unit, low_state(way, unit))

            @pl.when(takes_any(way))
            def _():
                forward(way, j, other_unit(j)).wait_recv()

            @pl.when(jnp.logical_not(gives_inner(way)))
            def _():
                to_partner(way, half + j).wait_recv()

            use(other_unit(j), low_state(way, other_unit(j)))
            return carry

        lax.fori_loop(0, half, step, 0)

    def low_state(way, unit):
        state = outer[way, states(unit)]
        state = jnp.where(gives_inner(way), state, state + inner_in[way, states(unit)])
        state = state.astype(BF16)
        return block_diagonal(state[0], state[1])

    def end_sends(way):
        def step(j, carry):
            to_partner(way, j).wait_send()

            @pl.when(gives_inner(way))
            def _():
                to_partner(way, half + j).wait_send()

            for d in range(1, chips):

                @pl.when(sends_to(way, d))
                def _():
                    across(way, d, j).wait_send()

            @pl.when(takes_any(way))
            def _():
                forward(way, j, own_unit(j)).wait_send()

            return carry

        lax.fori_loop(0, half, step, 0)

    def make_kv(i, unit):
        load(i, 0).wait()
        load(i, 1).wait()
        key, value = k[:, cols(unit)], v[:, cols(unit)]
        for n in range(2):
            at = slice(n * HD, (n + 1) * HD)
            local[0, 2 * unit + n] = dot(key[:, at], value[:, at], 0, 0)

    send_states(0, make_kv)
    load_q.start()
    load_ct.start()

    causal = lax.broadcasted_iota(jnp.int32, (tile, tile), 0) >= lax.broadcasted_iota(
        jnp.int32, (tile, tile), 1
    )

    def masked(scores):
        return jnp.where(causal, scores, 0.0).astype(BF16)

    acc_sq[...] = jnp.zeros_like(acc_sq)
    acc_in[...] = jnp.zeros_like(acc_in)
    load_q.wait()

    def own_scores(unit, carry):
        query, key, value = q[:, cols(unit)], k[:, cols(unit)], v[:, cols(unit)]
        for n in range(2):
            at = slice(n * HD, (n + 1) * HD)
            qh, kh, vh = query[:, at], key[:, at], value[:, at]
            w00 = masked(dot(qh[:tile], kh[:tile], 1, 1))
            w10 = dot(qh[tile:], kh[:tile], 1, 1).astype(BF16)
            w11 = masked(dot(qh[tile:], kh[tile:], 1, 1))
            weights[2 * unit + n, 0] = w00
            weights[2 * unit + n, 1] = w10
            weights[2 * unit + n, 2] = w11
            where = pl.ds(pl.multiple_of(unit * PAIR + n * HD, HD), HD)
            att[:tile, where] = dot(w00, vh[:tile], 1, 0)
            att[tile:, where] = dot(jnp.concatenate([w10, w11], axis=1), vh, 1, 0)
        return carry

    lax.fori_loop(0, units, own_scores, 0)
    load_ct.wait()

    def add_prefix(unit, low):
        prefix[unit] = low
        attended = att[:, cols(unit)] + dot(q[:, cols(unit)], low, 1, 0)
        att[:, cols(unit)] = attended
        squared = attended * attended
        product = ct[:, cols(unit)].astype(F32) * gain_ref[:, cols(unit)] * attended
        acc_sq[...] += squared[:, :HD] + squared[:, HD:]
        acc_in[...] += product[:, :HD] + product[:, HD:]

    take_states(0, add_prefix)

    stat_out[0:1, :] = jnp.sum(acc_sq[...].T, axis=0, keepdims=True)
    stat_out[1:2, :] = jnp.sum(acc_in[...].T, axis=0, keepdims=True)
    stat_out[2:8, :] = jnp.zeros((6, tokens), F32)

    def stat_copy(d):
        return pltpu.make_async_remote_copy(
            src_ref=stat_out,
            dst_ref=stat_in.at[d - 1],
            send_sem=stat_send.at[d - 1],
            recv_sem=stat_recv.at[d - 1],
            device_id={"head": lax.rem(head + d, head_size)},
            device_id_type=MESH,
        )

    for d in range(1, head_size):
        stat_copy(d).start()
    sums = stat_out[...]
    for d in range(1, head_size):
        stat_copy(d).wait_recv()
        sums = sums + stat_in[d - 1]
    inverse = lax.rsqrt(sums[0:1] / FEAT + EPS)
    scale = sums[1:2] * inverse * inverse * inverse / FEAT
    acc_sq[...] = jnp.broadcast_to(inverse, (HD, tokens)).T
    acc_in[...] = jnp.broadcast_to(scale, (HD, tokens)).T

    def make_qg(i, unit):
        gain = gain_ref[:, cols(unit)]
        inv = jnp.concatenate([acc_sq[...]] * 2, axis=1)
        coef = jnp.concatenate([acc_in[...]] * 2, axis=1)
        attended = att[:, cols(unit)]
        scaled = ct[:, cols(unit)].astype(F32) * gain
        out_grad = (inv * scaled - attended * coef).astype(BF16)
        og[:, cols(unit)] = out_grad
        query = q[:, cols(unit)]
        for n in range(2):
            at = slice(n * HD, (n + 1) * HD)
            local[1, 2 * unit + n] = dot(query[:, at], out_grad[:, at], 0, 0)

    send_states(1, make_qg)

    def finish_forward(unit, carry):
        inv = jnp.concatenate([acc_sq[...]] * 2, axis=1)
        lo[:, cols(unit)] = (att[:, cols(unit)] * inv * gain_ref[:, cols(unit)]).astype(BF16)
        return carry

    lax.fori_loop(0, units, finish_forward, 0)
    part_k = att

    def own_grads(unit, carry):
        query, key, value = q[:, cols(unit)], k[:, cols(unit)], v[:, cols(unit)]
        grad = og[:, cols(unit)]
        from_prefix = dot(grad, prefix[unit], 1, 1)
        for n in range(2):
            at = slice(n * HD, (n + 1) * HD)
            qh, kh, vh, gh = query[:, at], key[:, at], value[:, at], grad[:, at]
            g00 = masked(dot(gh[:tile], vh[:tile], 1, 1))
            g10 = dot(gh[tile:], vh[:tile], 1, 1).astype(BF16)
            g11 = masked(dot(gh[tile:], vh[tile:], 1, 1))
            w00 = weights[2 * unit + n, 0]
            w10 = weights[2 * unit + n, 1]
            w11 = weights[2 * unit + n, 2]
            where = pl.ds(pl.multiple_of(unit * PAIR + n * HD, HD), HD)
            gq[:tile, where] = (from_prefix[:tile, at] + dot(g00, kh[:tile], 1, 0)).astype(BF16)
            gq[tile:, where] = (
                from_prefix[tile:, at] + dot(jnp.concatenate([g10, g11], axis=1), kh, 1, 0)
            ).astype(BF16)
            part_k[:tile, where] = dot(jnp.concatenate([g00, g10], axis=0), qh, 0, 0)
            part_k[tile:, where] = dot(g11, qh[tile:], 0, 0)
            part_v[:tile, where] = dot(jnp.concatenate([w00, w10], axis=0), gh, 0, 0)
            part_v[tile:, where] = dot(w11, gh[tile:], 0, 0)
        return carry

    lax.fori_loop(0, units, own_grads, 0)

    def add_suffix(unit, low):
        at = cols(unit)
        gk[:, at] = (part_k[:, at] + dot(v[:, at], low, 1, 1)).astype(BF16)
        gv[:, at] = (part_v[:, at] + dot(k[:, at], low, 1, 0)).astype(BF16)

    take_states(1, add_suffix)

    end_sends(0)
    end_sends(1)
    for d in range(1, head_size):
        stat_copy(d).wait_send()


def per_device(seq_size, head_size, queries, key_vectors, value_vectors, norm_gain, cotangent):
    tokens, columns = queries.shape
    heads = columns // HD
    units = heads // 2
    half = units // 2
    chips = seq_size // 2
    dma = pltpu.SemaphoreType.DMA
    in_hbm = pl.BlockSpec(memory_space=pltpu.HBM)
    narrow = pltpu.VMEM((tokens, columns), BF16)
    wide = pltpu.VMEM((tokens, columns), F32)
    return pl.pallas_call(
        functools.partial(kernel, seq_size, head_size),
        out_shape=(narrow,) * 4,
        in_specs=[in_hbm] * 3 + [pl.BlockSpec(memory_space=pltpu.VMEM), in_hbm],
        out_specs=(pl.BlockSpec(memory_space=pltpu.VMEM),) * 4,
        scratch_shapes=[narrow] * 4
        + [
            pltpu.VMEM((heads, 3, tokens // 2, tokens // 2), BF16),
            wide,
            narrow,
            wide,
            pltpu.VMEM((2, heads, HD, HD), F32),
            pltpu.VMEM((2, heads, HD, HD), F32),
            pltpu.VMEM((2, heads // 2, HD, HD), F32),
            pltpu.VMEM((2, max(chips - 1, 1), heads // 2, HD, HD), F32),
            pltpu.VMEM((2, heads, HD, HD), F32),
            pltpu.VMEM((units, PAIR, PAIR), BF16),
            pltpu.VMEM((tokens, HD), F32),
            pltpu.VMEM((tokens, HD), F32),
            pltpu.VMEM((8, tokens), F32),
            pltpu.VMEM((max(head_size - 1, 1), 8, tokens), F32),
            dma((2, units)),
            dma((2,)),
            dma((2, units)),
            dma((2, units)),
            dma((2, max(chips - 1, 1), half)),
            dma((2, max(chips - 1, 1), half)),
            dma((2, half)),
            dma((2, half)),
            dma((max(head_size - 1, 1),)),
            dma((max(head_size - 1, 1),)),
        ],
        compiler_params=pltpu.CompilerParams(
            collective_id=0, has_side_effects=True, vmem_limit_bytes=48 * 1024 * 1024
        ),
        cost_estimate=pl.CostEstimate(
            flops=12 * tokens * tokens * columns,
            bytes_accessed=16 * tokens * columns,
            transcendentals=tokens,
        ),
    )(queries, key_vectors, value_vectors, norm_gain.reshape(1, columns), cotangent)


def solution(mesh):
    rows, features = P(("dp", "seq"), "head"), P("head")
    return jax.shard_map(
        functools.partial(per_device, mesh.shape["seq"], mesh.shape["head"]),
        mesh=mesh,
        in_specs=(rows, rows, rows, features, rows),
        out_specs=(rows,) * 4,
        check_vma=False,
    )
```

```python
import functools

import jax
import jax.numpy as jnp
from jax import lax
from jax.experimental import pallas as pl
from jax.experimental.pallas import tpu as pltpu
from jax.sharding import PartitionSpec as P

HD = 128
PAIR = 2 * HD
FEAT = 4096
EPS = 1e-06
MESH = pl.DeviceIdType.MESH
F32 = jnp.float32
BF16 = jnp.bfloat16


def dot(a, b, a_dim, b_dim):
    return lax.dot_general(a, b, (((a_dim,), (b_dim,)), ((), ())), preferred_element_type=F32)


def block_diagonal(first, second):
    empty = jnp.zeros_like(first)
    return jnp.concatenate(
        [jnp.concatenate([first, empty], axis=1), jnp.concatenate([empty, second], axis=1)], axis=0
    )


def kernel(
    seq_size, head_size,
    q_hbm, k_hbm, v_hbm, gain_ref, ct_hbm,
    lo, gq, gk, gv,
    q, k, v, ct,
    weights, q_turned, att, og, part_v,
    local, inner_in, total, cross_in, outer, prefix, acc_sq, acc_in, stat_out, stat_in,
    kv_sem, in_sem,
    in_send, in_recv, cross_send, cross_recv, fwd_send, fwd_recv, stat_send, stat_recv,
):
    tokens, columns = q.shape
    tile = tokens // 2
    units = columns // PAIR
    half = units // 2
    chips = seq_size // 2
    me = lax.axis_index("seq")
    chip, core = me // 2, me % 2
    head = lax.axis_index("head")
    partner = chip * 2 + 1 - core

    def cols(unit):
        return pl.ds(pl.multiple_of(unit * PAIR, PAIR), PAIR)

    def own_unit(j):
        return core * half + j

    def other_unit(j):
        return (1 - core) * half + j

    def load(i, which):
        unit = lax.rem((1 - core) * half + i, units)
        source, target = ((k_hbm, k), (v_hbm, v))[which]
        return pltpu.make_async_copy(
            source.at[:, cols(unit)], target.at[:, cols(unit)], kv_sem.at[which, i]
        )

    def start_load(i, carry):
        for n in (i, half + i):
            load(n, 0).start()
            load(n, 1).start()
        return carry

    lax.fori_loop(0, half, start_load, 0)
    load_q = pltpu.make_async_copy(q_hbm, q, in_sem.at[0])
    load_ct = pltpu.make_async_copy(ct_hbm, ct, in_sem.at[1])

    barrier = pltpu.get_barrier_semaphore()
    pl.semaphore_signal(barrier, inc=1, device_id={"seq": partner}, device_id_type=MESH)
    for d in range(1, chips):
        pl.semaphore_signal(
            barrier, inc=1, device_id={"seq": lax.rem(me + 2 * d, seq_size)}, device_id_type=MESH
        )
    for d in range(1, head_size):
        pl.semaphore_signal(
            barrier, inc=1, device_id={"head": lax.rem(head + d, head_size)}, device_id_type=MESH
        )
    pl.semaphore_wait(barrier, 1 + (chips - 1) + (head_size - 1))

    def states(unit):
        return pl.ds(2 * unit, 2)

    def to_partner(way, i):
        unit = lax.rem((1 - core) * half + i, units)
        return pltpu.make_async_remote_copy(
            src_ref=local.at[way, states(unit)],
            dst_ref=inner_in.at[way, states(unit)],
            send_sem=in_send.at[way, i],
            recv_sem=in_recv.at[way, i],
            device_id={"seq": partner},
            device_id_type=MESH,
        )

    def across(way, d, j):
        step = 2 * d if way == 0 else -2 * d
        return pltpu.make_async_remote_copy(
            src_ref=total.at[way, states(j)],
            dst_ref=cross_in.at[way, d - 1, states(j)],
            send_sem=cross_send.at[way, d - 1, j],
            recv_sem=cross_recv.at[way, d - 1, j],
            device_id={"seq": lax.rem(me + step + seq_size, seq_size)},
            device_id_type=MESH,
        )

    def forward(way, j, unit):
        return pltpu.make_async_remote_copy(
            src_ref=outer.at[way, states(unit)],
            dst_ref=outer.at[way, states(unit)],
            send_sem=fwd_send.at[way, j],
            recv_sem=fwd_recv.at[way, j],
            device_id={"seq": partner},
            device_id_type=MESH,
        )

    def sends_to(way, d):
        return chip + d < chips if way == 0 else chip - d >= 0

    def takes_from(way, d):
        return chip - d >= 0 if way == 0 else chip + d < chips

    def takes_any(way):
        return chip > 0 if way == 0 else chip < chips - 1

    def gives_inner(way):
        return core == 0 if way == 0 else core == 1

    def send_states(way, make):
        def give_other(i):
            make(i, other_unit(i))
            to_partner(way, i).start()

        give_other(0)

        def step(j, carry):
            unit = own_unit(j)
            make(half + j, unit)

            @pl.when(gives_inner(way))
            def _():
                to_partner(way, half + j).start()

            @pl.when(j + 1 < half)
            def _():
                give_other(j + 1)

            to_partner(way, j).wait_recv()
            total[way, states(j)] = local[way, states(unit)] + inner_in[way, states(unit)]
            for d in range(1, chips):

                @pl.when(sends_to(way, d))
                def _():
                    across(way, d, j).start()

            return carry

        lax.fori_loop(0, half, step, 0)

    def take_states(way, use):
        def step(j, carry):
            unit = own_unit(j)

            @pl.when(takes_any(way))
            def _():
                outer[way, states(unit)] = jnp.zeros((2, HD, HD), F32)
                for d in range(1, chips):

                    @pl.when(takes_from(way, d))
                    def _():
                        across(way, d, j).wait_recv()
                        outer[way, states(unit)] += cross_in[way, d - 1, states(j)]

                forward(way, j, unit).start()

            @pl.when(jnp.logical_not(takes_any(way)))
            def _():
                outer[way, states(unit)] = jnp.zeros((2, HD, HD), F32)
                outer[way, states(other_unit(j))] = jnp.zeros((2, HD, HD), F32)

            use(unit, low_state(way, unit))

            @pl.when(takes_any(way))
            def _():
                forward(way, j, other_unit(j)).wait_recv()

            @pl.when(jnp.logical_not(gives_inner(way)))
            def _():
                to_partner(way, half + j).wait_recv()

            use(other_unit(j), low_state(way, other_unit(j)))
            return carry

        lax.fori_loop(0, half, step, 0)

    def low_state(way, unit):
        state = outer[way, states(unit)]
        state = jnp.where(gives_inner(way), state, state + inner_in[way, states(unit)])
        state = state.astype(BF16)
        return block_diagonal(state[0], state[1])

    def end_sends(way):
        def step(j, carry):
            to_partner(way, j).wait_send()

            @pl.when(gives_inner(way))
            def _():
                to_partner(way, half + j).wait_send()

            for d in range(1, chips):

                @pl.when(sends_to(way, d))
                def _():
                    across(way, d, j).wait_send()

            @pl.when(takes_any(way))
            def _():
                forward(way, j, own_unit(j)).wait_send()

            return carry

        lax.fori_loop(0, half, step, 0)

    def make_kv(i, unit):
        load(i, 0).wait()
        load(i, 1).wait()
        key, value = k[:, cols(unit)], v[:, cols(unit)]
        for n in range(2):
            at = slice(n * HD, (n + 1) * HD)
            local[0, 2 * unit + n] = dot(key[:, at], value[:, at], 0, 0)

    send_states(0, make_kv)
    load_q.start()
    load_ct.start()

    row = lax.broadcasted_iota(jnp.int32, (tile, tile), 0)
    column = lax.broadcasted_iota(jnp.int32, (tile, tile), 1)

    acc_sq[...] = jnp.zeros_like(acc_sq)
    acc_in[...] = jnp.zeros_like(acc_in)
    load_q.wait()

    def own_scores(unit, carry):
        query, key, value = q[:, cols(unit)], k[:, cols(unit)], v[:, cols(unit)]
        for n in range(2):
            at = slice(n * HD, (n + 1) * HD)
            qh, kh, vh = query[:, at], key[:, at], value[:, at]
            w00 = jnp.where(row <= column, dot(kh[:tile], qh[:tile], 1, 1), 0.0).astype(BF16)
            w01 = dot(kh[:tile], qh[tile:], 1, 1).astype(BF16)
            w11 = jnp.where(row <= column, dot(kh[tile:], qh[tile:], 1, 1), 0.0).astype(BF16)
            weights[2 * unit + n, 0] = w00
            weights[2 * unit + n, 1] = w01
            weights[2 * unit + n, 2] = w11
            where = pl.ds(pl.multiple_of(unit * PAIR + n * HD, HD), HD)
            att[:tile, where] = dot(w00, vh[:tile], 0, 0)
            att[tile:, where] = dot(jnp.concatenate([w01, w11], axis=0), vh, 0, 0)
        q_turned[unit] = query.T
        return carry

    lax.fori_loop(0, units, own_scores, 0)
    load_ct.wait()

    def add_prefix(unit, low):
        prefix[unit] = low
        attended = att[:, cols(unit)] + dot(q[:, cols(unit)], low, 1, 0)
        att[:, cols(unit)] = attended
        squared = attended * attended
        product = ct[:, cols(unit)].astype(F32) * gain_ref[:, cols(unit)] * attended
        acc_sq[...] += squared[:, :HD] + squared[:, HD:]
        acc_in[...] += product[:, :HD] + product[:, HD:]

    take_states(0, add_prefix)

    stat_out[0:1, :] = jnp.sum(acc_sq[...].T, axis=0, keepdims=True)
    stat_out[1:2, :] = jnp.sum(acc_in[...].T, axis=0, keepdims=True)
    stat_out[2:8, :] = jnp.zeros((6, tokens), F32)

    def stat_copy(d):
        return pltpu.make_async_remote_copy(
            src_ref=stat_out,
            dst_ref=stat_in.at[d - 1],
            send_sem=stat_send.at[d - 1],
            recv_sem=stat_recv.at[d - 1],
            device_id={"head": lax.rem(head + d, head_size)},
            device_id_type=MESH,
        )

    for d in range(1, head_size):
        stat_copy(d).start()
    sums = stat_out[...]
    for d in range(1, head_size):
        stat_copy(d).wait_recv()
        sums = sums + stat_in[d - 1]
    inverse = lax.rsqrt(sums[0:1] / FEAT + EPS)
    scale = sums[1:2] * inverse * inverse * inverse / FEAT
    acc_sq[...] = jnp.broadcast_to(inverse, (HD, tokens)).T
    acc_in[...] = jnp.broadcast_to(scale, (HD, tokens)).T

    def make_qg(i, unit):
        gain = gain_ref[:, cols(unit)]
        inv = jnp.concatenate([acc_sq[...]] * 2, axis=1)
        coef = jnp.concatenate([acc_in[...]] * 2, axis=1)
        attended = att[:, cols(unit)]
        scaled = ct[:, cols(unit)].astype(F32) * gain
        out_grad = (inv * scaled - attended * coef).astype(BF16)
        og[:, cols(unit)] = out_grad
        turned = q_turned[unit]
        for n in range(2):
            at = slice(n * HD, (n + 1) * HD)
            local[1, 2 * unit + n] = dot(turned[at], out_grad[:, at], 1, 0)

    send_states(1, make_qg)

    part_k = att

    def own_grads(unit, carry):
        query, key, value = q[:, cols(unit)], k[:, cols(unit)], v[:, cols(unit)]
        grad = og[:, cols(unit)]
        inv = jnp.concatenate([acc_sq[...]] * 2, axis=1)
        lo[:, cols(unit)] = (att[:, cols(unit)] * inv * gain_ref[:, cols(unit)]).astype(BF16)
        from_prefix = dot(grad, prefix[unit], 1, 1)
        for n in range(2):
            at = slice(n * HD, (n + 1) * HD)
            qh, kh, vh, gh = query[:, at], key[:, at], value[:, at], grad[:, at]
            g00 = jnp.where(row >= column, dot(gh[:tile], vh[:tile], 1, 1), 0.0).astype(BF16)
            g10 = dot(gh[tile:], vh[:tile], 1, 1).astype(BF16)
            g11 = jnp.where(row >= column, dot(gh[tile:], vh[tile:], 1, 1), 0.0).astype(BF16)
            w00 = weights[2 * unit + n, 0]
            w01 = weights[2 * unit + n, 1]
            w11 = weights[2 * unit + n, 2]
            where = pl.ds(pl.multiple_of(unit * PAIR + n * HD, HD), HD)
            gq[:tile, where] = (from_prefix[:tile, at] + dot(g00, kh[:tile], 1, 0)).astype(BF16)
            gq[tile:, where] = (
                from_prefix[tile:, at] + dot(jnp.concatenate([g10, g11], axis=1), kh, 1, 0)
            ).astype(BF16)
            part_k[:tile, where] = dot(jnp.concatenate([g00, g10], axis=0), qh, 0, 0)
            part_k[tile:, where] = dot(g11, qh[tile:], 0, 0)
            part_v[:tile, where] = dot(jnp.concatenate([w00, w01], axis=1), gh, 1, 0)
            part_v[tile:, where] = dot(w11, gh[tile:], 1, 0)
        return carry

    lax.fori_loop(0, units, own_grads, 0)

    def add_suffix(unit, low):
        at = cols(unit)
        gk[:, at] = (part_k[:, at] + dot(v[:, at], low, 1, 1)).astype(BF16)
        gv[:, at] = (part_v[:, at] + dot(k[:, at], low, 1, 0)).astype(BF16)

    take_states(1, add_suffix)

    end_sends(0)
    end_sends(1)
    for d in range(1, head_size):
        stat_copy(d).wait_send()


def write_out(*refs):
    sources, targets, sems = refs[:4], refs[4:8], refs[8]
    rows = sources[0].shape[0] // 4
    copies = [
        pltpu.make_async_copy(
            source.at[pl.ds(part * rows, rows)], target.at[pl.ds(part * rows, rows)], sems.at[n, part]
        )
        for part in range(4)
        for n, (source, target) in enumerate(zip(sources, targets))
    ]
    for copy in copies:
        copy.start()
    for copy in copies:
        copy.wait()


def per_device(seq_size, head_size, queries, key_vectors, value_vectors, norm_gain, cotangent):
    tokens, columns = queries.shape
    heads = columns // HD
    units = heads // 2
    half = units // 2
    chips = seq_size // 2
    dma = pltpu.SemaphoreType.DMA
    in_hbm = pl.BlockSpec(memory_space=pltpu.HBM)
    narrow = pltpu.VMEM((tokens, columns), BF16)
    wide = pltpu.VMEM((tokens, columns), F32)
    results = pl.pallas_call(
        functools.partial(kernel, seq_size, head_size),
        out_shape=(narrow,) * 4,
        in_specs=[in_hbm] * 3 + [pl.BlockSpec(memory_space=pltpu.VMEM), in_hbm],
        out_specs=(pl.BlockSpec(memory_space=pltpu.VMEM),) * 4,
        scratch_shapes=[narrow] * 4
        + [
            pltpu.VMEM((heads, 3, tokens // 2, tokens // 2), BF16),
            pltpu.VMEM((units, PAIR, tokens), BF16),
            wide,
            narrow,
            wide,
            pltpu.VMEM((2, heads, HD, HD), F32),
            pltpu.VMEM((2, heads, HD, HD), F32),
            pltpu.VMEM((2, heads // 2, HD, HD), F32),
            pltpu.VMEM((2, max(chips - 1, 1), heads // 2, HD, HD), F32),
            pltpu.VMEM((2, heads, HD, HD), F32),
            pltpu.VMEM((units, PAIR, PAIR), BF16),
            pltpu.VMEM((tokens, HD), F32),
            pltpu.VMEM((tokens, HD), F32),
            pltpu.VMEM((8, tokens), F32),
            pltpu.VMEM((max(head_size - 1, 1), 8, tokens), F32),
            dma((2, units)),
            dma((2,)),
            dma((2, units)),
            dma((2, units)),
            dma((2, max(chips - 1, 1), half)),
            dma((2, max(chips - 1, 1), half)),
            dma((2, half)),
            dma((2, half)),
            dma((max(head_size - 1, 1),)),
            dma((max(head_size - 1, 1),)),
        ],
        compiler_params=pltpu.CompilerParams(
            collective_id=0, has_side_effects=True, vmem_limit_bytes=48 * 1024 * 1024
        ),
        cost_estimate=pl.CostEstimate(
            flops=12 * tokens * tokens * columns,
            bytes_accessed=16 * tokens * columns,
            transcendentals=tokens,
        ),
    )(queries, key_vectors, value_vectors, norm_gain.reshape(1, columns), cotangent)
    out = jax.ShapeDtypeStruct((tokens, columns), BF16)
    return pl.pallas_call(
        write_out,
        out_shape=(out,) * 4,
        in_specs=[pl.BlockSpec(memory_space=pltpu.VMEM)] * 4,
        out_specs=(pl.BlockSpec(memory_space=pltpu.HBM),) * 4,
        scratch_shapes=[dma((4, 4))],
        cost_estimate=pl.CostEstimate(
            flops=0, bytes_accessed=8 * tokens * columns, transcendentals=0
        ),
    )(*results)


def solution(mesh):
    rows, features = P(("dp", "seq"), "head"), P("head")
    return jax.shard_map(
        functools.partial(per_device, mesh.shape["seq"], mesh.shape["head"]),
        mesh=mesh,
        in_specs=(rows, rows, rows, features, rows),
        out_specs=(rows,) * 4,
        check_vma=False,
    )
```

```python
import functools

import jax
import jax.numpy as jnp
from jax import lax
from jax.experimental import pallas as pl
from jax.experimental.pallas import tpu as pltpu
from jax.sharding import PartitionSpec as P

HD = 128
PAIR = 2 * HD
FEAT = 4096
EPS = 1e-06
MESH = pl.DeviceIdType.MESH
F32 = jnp.float32
BF16 = jnp.bfloat16


def dot(a, b, a_dim, b_dim):
    return lax.dot_general(a, b, (((a_dim,), (b_dim,)), ((), ())), preferred_element_type=F32)


def block_diagonal(first, second):
    empty = jnp.zeros_like(first)
    return jnp.concatenate(
        [jnp.concatenate([first, empty], axis=1), jnp.concatenate([empty, second], axis=1)], axis=0
    )


def kernel(
    seq_size, head_size,
    q_hbm, k_hbm, v_hbm, gain_ref, ct_hbm,
    lo, gq, gk, gv,
    q, k, v, ct,
    weights, att, og, part_v,
    local, inner_in, total, cross_in, outer, prefix, acc_sq, acc_in, stat_out, stat_in,
    kv_sem, in_sem,
    in_send, in_recv, cross_send, cross_recv, fwd_send, fwd_recv, stat_send, stat_recv,
):
    tokens, columns = q.shape
    tile = tokens // 2
    units = columns // PAIR
    half = units // 2
    chips = seq_size // 2
    me = lax.axis_index("seq")
    chip, core = me // 2, me % 2
    head = lax.axis_index("head")
    partner = chip * 2 + 1 - core

    def cols(unit):
        return pl.ds(pl.multiple_of(unit * PAIR, PAIR), PAIR)

    def own_unit(j):
        return core * half + j

    def other_unit(j):
        return (1 - core) * half + j

    def load(i, which):
        unit = lax.rem((1 - core) * half + i, units)
        source, target = ((k_hbm, k), (v_hbm, v))[which]
        return pltpu.make_async_copy(
            source.at[:, cols(unit)], target.at[:, cols(unit)], kv_sem.at[which, i]
        )

    def start_load(i, carry):
        for n in (i, half + i):
            load(n, 0).start()
            load(n, 1).start()
        return carry

    lax.fori_loop(0, half, start_load, 0)
    load_q = pltpu.make_async_copy(q_hbm, q, in_sem.at[0])
    load_ct = pltpu.make_async_copy(ct_hbm, ct, in_sem.at[1])
    load_q.start()
    load_ct.start()

    barrier = pltpu.get_barrier_semaphore()
    pl.semaphore_signal(barrier, inc=1, device_id={"seq": partner}, device_id_type=MESH)
    for d in range(1, chips):
        pl.semaphore_signal(
            barrier, inc=1, device_id={"seq": lax.rem(me + 2 * d, seq_size)}, device_id_type=MESH
        )
    for d in range(1, head_size):
        pl.semaphore_signal(
            barrier, inc=1, device_id={"head": lax.rem(head + d, head_size)}, device_id_type=MESH
        )
    pl.semaphore_wait(barrier, 1 + (chips - 1) + (head_size - 1))

    def states(unit):
        return pl.ds(2 * unit, 2)

    def to_partner(way, i):
        unit = lax.rem((1 - core) * half + i, units)
        return pltpu.make_async_remote_copy(
            src_ref=local.at[way, states(unit)],
            dst_ref=inner_in.at[way, states(unit)],
            send_sem=in_send.at[way, i],
            recv_sem=in_recv.at[way, i],
            device_id={"seq": partner},
            device_id_type=MESH,
        )

    def across(way, d, j):
        step = 2 * d if way == 0 else -2 * d
        return pltpu.make_async_remote_copy(
            src_ref=total.at[way, states(j)],
            dst_ref=cross_in.at[way, d - 1, states(j)],
            send_sem=cross_send.at[way, d - 1, j],
            recv_sem=cross_recv.at[way, d - 1, j],
            device_id={"seq": lax.rem(me + step + seq_size, seq_size)},
            device_id_type=MESH,
        )

    def forward(way, j, unit):
        return pltpu.make_async_remote_copy(
            src_ref=outer.at[way, states(unit)],
            dst_ref=outer.at[way, states(unit)],
            send_sem=fwd_send.at[way, j],
            recv_sem=fwd_recv.at[way, j],
            device_id={"seq": partner},
            device_id_type=MESH,
        )

    def sends_to(way, d):
        return chip + d < chips if way == 0 else chip - d >= 0

    def takes_from(way, d):
        return chip - d >= 0 if way == 0 else chip + d < chips

    def takes_any(way):
        return chip > 0 if way == 0 else chip < chips - 1

    def gives_inner(way):
        return core == 0 if way == 0 else core == 1

    def send_states(way, make):
        def give_other(i):
            make(i, other_unit(i))
            to_partner(way, i).start()

        give_other(0)

        def step(j, carry):
            unit = own_unit(j)
            make(half + j, unit)

            @pl.when(gives_inner(way))
            def _():
                to_partner(way, half + j).start()

            @pl.when(j + 1 < half)
            def _():
                give_other(j + 1)

            to_partner(way, j).wait_recv()
            total[way, states(j)] = local[way, states(unit)] + inner_in[way, states(unit)]
            for d in range(1, chips):

                @pl.when(sends_to(way, d))
                def _():
                    across(way, d, j).start()

            return carry

        lax.fori_loop(0, half, step, 0)

    def take_states(way, use):
        def step(j, carry):
            unit = own_unit(j)

            @pl.when(takes_any(way))
            def _():
                outer[way, states(unit)] = jnp.zeros((2, HD, HD), F32)
                for d in range(1, chips):

                    @pl.when(takes_from(way, d))
                    def _():
                        across(way, d, j).wait_recv()
                        outer[way, states(unit)] += cross_in[way, d - 1, states(j)]

                forward(way, j, unit).start()

            @pl.when(jnp.logical_not(takes_any(way)))
            def _():
                outer[way, states(unit)] = jnp.zeros((2, HD, HD), F32)
                outer[way, states(other_unit(j))] = jnp.zeros((2, HD, HD), F32)

            use(unit, low_state(way, unit))

            @pl.when(takes_any(way))
            def _():
                forward(way, j, other_unit(j)).wait_recv()

            @pl.when(jnp.logical_not(gives_inner(way)))
            def _():
                to_partner(way, half + j).wait_recv()

            use(other_unit(j), low_state(way, other_unit(j)))
            return carry

        lax.fori_loop(0, half, step, 0)

    def low_state(way, unit):
        state = outer[way, states(unit)]
        state = jnp.where(gives_inner(way), state, state + inner_in[way, states(unit)])
        state = state.astype(BF16)
        return block_diagonal(state[0], state[1])

    def end_sends(way):
        def step(j, carry):
            to_partner(way, j).wait_send()

            @pl.when(gives_inner(way))
            def _():
                to_partner(way, half + j).wait_send()

            for d in range(1, chips):

                @pl.when(sends_to(way, d))
                def _():
                    across(way, d, j).wait_send()

            @pl.when(takes_any(way))
            def _():
                forward(way, j, own_unit(j)).wait_send()

            return carry

        lax.fori_loop(0, half, step, 0)

    def put_state(way, unit, both):
        local[way, 2 * unit] = both[:HD, :HD]
        local[way, 2 * unit + 1] = both[HD:, HD:]

    def make_kv(i, unit):
        load(i, 0).wait()
        load(i, 1).wait()
        put_state(0, unit, dot(k[:, cols(unit)], v[:, cols(unit)], 0, 0))

    send_states(0, make_kv)

    def causal(scores):
        row = lax.broadcasted_iota(jnp.int32, (tile, tile), 0)
        column = lax.broadcasted_iota(jnp.int32, (tile, tile), 1)
        return jnp.where(row >= column, scores, 0.0).astype(BF16)

    def three_tiles(rows, columns):
        left = dot(rows, columns[:tile], 1, 1)
        right = dot(rows[tile:], columns[tile:], 1, 1)
        return causal(left[:tile]), left[tile:].astype(BF16), causal(right)

    def times(tiles, values):
        t00, t10, t11 = tiles
        first = dot(jnp.concatenate([t00, t10], axis=0), values[:tile], 1, 0)
        return first[:tile], first[tile:] + dot(t11, values[tile:], 1, 0)

    def turned_times(tiles, values):
        t00, t10, t11 = tiles
        second = dot(jnp.concatenate([t10, t11], axis=1), values[tile:], 0, 0)
        return second[:tile] + dot(t00, values[:tile], 0, 0), second[tile:]

    acc_sq[...] = jnp.zeros_like(acc_sq)
    acc_in[...] = jnp.zeros_like(acc_in)
    load_q.wait()

    def own_scores(unit, carry):
        query, key, value = q[:, cols(unit)], k[:, cols(unit)], v[:, cols(unit)]
        for n in range(2):
            at = slice(n * HD, (n + 1) * HD)
            qh, kh, vh = query[:, at], key[:, at], value[:, at]
            tiles = three_tiles(qh, kh)
            for m in range(3):
                weights[2 * unit + n, m] = tiles[m]
            where = pl.ds(pl.multiple_of(unit * PAIR + n * HD, HD), HD)
            att[:tile, where], att[tile:, where] = times(tiles, vh)
        return carry

    lax.fori_loop(0, units, own_scores, 0, unroll=2)
    load_ct.wait()

    def add_prefix(unit, low):
        prefix[unit] = low
        attended = att[:, cols(unit)] + dot(q[:, cols(unit)], low, 1, 0)
        att[:, cols(unit)] = attended
        squared = attended * attended
        product = ct[:, cols(unit)].astype(F32) * gain_ref[:, cols(unit)] * attended
        acc_sq[...] += squared[:, :HD] + squared[:, HD:]
        acc_in[...] += product[:, :HD] + product[:, HD:]

    take_states(0, add_prefix)

    stat_out[0:1, :] = jnp.sum(acc_sq[...].T, axis=0, keepdims=True)
    stat_out[1:2, :] = jnp.sum(acc_in[...].T, axis=0, keepdims=True)
    stat_out[2:8, :] = jnp.zeros((6, tokens), F32)

    def stat_copy(d):
        return pltpu.make_async_remote_copy(
            src_ref=stat_out,
            dst_ref=stat_in.at[d - 1],
            send_sem=stat_send.at[d - 1],
            recv_sem=stat_recv.at[d - 1],
            device_id={"head": lax.rem(head + d, head_size)},
            device_id_type=MESH,
        )

    for d in range(1, head_size):
        stat_copy(d).start()
    sums = stat_out[...]
    for d in range(1, head_size):
        stat_copy(d).wait_recv()
        sums = sums + stat_in[d - 1]
    inverse = lax.rsqrt(sums[0:1] / FEAT + EPS)
    scale = sums[1:2] * inverse * inverse * inverse / FEAT
    acc_sq[...] = jnp.broadcast_to(inverse, (HD, tokens)).T
    acc_in[...] = jnp.broadcast_to(scale, (HD, tokens)).T

    def make_qg(i, unit):
        gain = gain_ref[:, cols(unit)]
        inv = jnp.concatenate([acc_sq[...]] * 2, axis=1)
        coef = jnp.concatenate([acc_in[...]] * 2, axis=1)
        attended = att[:, cols(unit)]
        scaled = ct[:, cols(unit)].astype(F32) * gain
        out_grad = (inv * scaled - attended * coef).astype(BF16)
        og[:, cols(unit)] = out_grad
        put_state(1, unit, dot(q[:, cols(unit)], out_grad, 0, 0))

    send_states(1, make_qg)

    part_k = att

    def own_grads(unit, carry):
        query, key, value = q[:, cols(unit)], k[:, cols(unit)], v[:, cols(unit)]
        grad = og[:, cols(unit)]
        inv = jnp.concatenate([acc_sq[...]] * 2, axis=1)
        lo[:, cols(unit)] = (att[:, cols(unit)] * inv * gain_ref[:, cols(unit)]).astype(BF16)
        from_prefix = dot(grad, prefix[unit], 1, 1)
        for n in range(2):
            at = slice(n * HD, (n + 1) * HD)
            qh, kh, vh, gh = query[:, at], key[:, at], value[:, at], grad[:, at]
            tiles = three_tiles(gh, vh)
            kept = [weights[2 * unit + n, m] for m in range(3)]
            where = pl.ds(pl.multiple_of(unit * PAIR + n * HD, HD), HD)
            upper, lower = times(tiles, kh)
            gq[:tile, where] = (from_prefix[:tile, at] + upper).astype(BF16)
            gq[tile:, where] = (from_prefix[tile:, at] + lower).astype(BF16)
            part_k[:tile, where], part_k[tile:, where] = turned_times(tiles, qh)
            part_v[:tile, where], part_v[tile:, where] = turned_times(kept, gh)
        return carry

    lax.fori_loop(0, units, own_grads, 0, unroll=2)

    def add_suffix(unit, low):
        at = cols(unit)
        gk[:, at] = (part_k[:, at] + dot(v[:, at], low, 1, 1)).astype(BF16)
        gv[:, at] = (part_v[:, at] + dot(k[:, at], low, 1, 0)).astype(BF16)

    take_states(1, add_suffix)

    end_sends(0)
    end_sends(1)
    for d in range(1, head_size):
        stat_copy(d).wait_send()


def write_out(*refs):
    sources, targets, sems = refs[:4], refs[4:8], refs[8]
    rows = sources[0].shape[0] // 4
    copies = [
        pltpu.make_async_copy(
            source.at[pl.ds(part * rows, rows)], target.at[pl.ds(part * rows, rows)], sems.at[n, part]
        )
        for part in range(4)
        for n, (source, target) in enumerate(zip(sources, targets))
    ]
    for copy in copies:
        copy.start()
    for copy in copies:
        copy.wait()


def per_device(seq_size, head_size, queries, key_vectors, value_vectors, norm_gain, cotangent):
    tokens, columns = queries.shape
    heads = columns // HD
    units = heads // 2
    half = units // 2
    chips = seq_size // 2
    dma = pltpu.SemaphoreType.DMA
    in_hbm = pl.BlockSpec(memory_space=pltpu.HBM)
    narrow = pltpu.VMEM((tokens, columns), BF16)
    wide = pltpu.VMEM((tokens, columns), F32)
    results = pl.pallas_call(
        functools.partial(kernel, seq_size, head_size),
        out_shape=(narrow,) * 4,
        in_specs=[in_hbm] * 3 + [pl.BlockSpec(memory_space=pltpu.VMEM), in_hbm],
        out_specs=(pl.BlockSpec(memory_space=pltpu.VMEM),) * 4,
        scratch_shapes=[narrow] * 4
        + [
            pltpu.VMEM((heads, 3, tokens // 2, tokens // 2), BF16),
            wide,
            narrow,
            wide,
            pltpu.VMEM((2, heads, HD, HD), F32),
            pltpu.VMEM((2, heads, HD, HD), F32),
            pltpu.VMEM((2, heads // 2, HD, HD), F32),
            pltpu.VMEM((2, max(chips - 1, 1), heads // 2, HD, HD), F32),
            pltpu.VMEM((2, heads, HD, HD), F32),
            pltpu.VMEM((units, PAIR, PAIR), BF16),
            pltpu.VMEM((tokens, HD), F32),
            pltpu.VMEM((tokens, HD), F32),
            pltpu.VMEM((8, tokens), F32),
            pltpu.VMEM((max(head_size - 1, 1), 8, tokens), F32),
            dma((2, units)),
            dma((2,)),
            dma((2, units)),
            dma((2, units)),
            dma((2, max(chips - 1, 1), half)),
            dma((2, max(chips - 1, 1), half)),
            dma((2, half)),
            dma((2, half)),
            dma((max(head_size - 1, 1),)),
            dma((max(head_size - 1, 1),)),
        ],
        compiler_params=pltpu.CompilerParams(
            collective_id=0, has_side_effects=True, vmem_limit_bytes=48 * 1024 * 1024
        ),
        cost_estimate=pl.CostEstimate(
            flops=12 * tokens * tokens * columns,
            bytes_accessed=16 * tokens * columns,
            transcendentals=tokens,
        ),
    )(queries, key_vectors, value_vectors, norm_gain.reshape(1, columns), cotangent)
    out = jax.ShapeDtypeStruct((tokens, columns), BF16)
    return pl.pallas_call(
        write_out,
        out_shape=(out,) * 4,
        in_specs=[pl.BlockSpec(memory_space=pltpu.VMEM)] * 4,
        compiler_params=pltpu.CompilerParams(vmem_limit_bytes=1024 * 1024),
        out_specs=(pl.BlockSpec(memory_space=pltpu.HBM),) * 4,
        scratch_shapes=[dma((4, 4))],
        cost_estimate=pl.CostEstimate(
            flops=0, bytes_accessed=8 * tokens * columns, transcendentals=0
        ),
    )(*results)


def solution(mesh):
    rows, features = P(("dp", "seq"), "head"), P("head")
    return jax.shard_map(
        functools.partial(per_device, mesh.shape["seq"], mesh.shape["head"]),
        mesh=mesh,
        in_specs=(rows, rows, rows, features, rows),
        out_specs=(rows,) * 4,
        check_vma=False,
    )
```

```python
import functools

import jax
import jax.numpy as jnp
from jax import lax
from jax.experimental import pallas as pl
from jax.experimental.pallas import tpu as pltpu
from jax.sharding import PartitionSpec as P

HD = 128
PAIR = 2 * HD
FEAT = 4096
EPS = 1e-06
MESH = pl.DeviceIdType.MESH
F32 = jnp.float32
BF16 = jnp.bfloat16


def dot(a, b, a_dim, b_dim):
    return lax.dot_general(a, b, (((a_dim,), (b_dim,)), ((), ())), preferred_element_type=F32)


def block_diagonal(first, second):
    empty = jnp.zeros_like(first)
    return jnp.concatenate(
        [jnp.concatenate([first, empty], axis=1), jnp.concatenate([empty, second], axis=1)], axis=0
    )


def kernel(
    seq_size, head_size,
    q_hbm, k_hbm, v_hbm, gain_ref, ct_hbm,
    lo, gq, gk, gv,
    q, k, v, ct,
    weights, att, og, part_v,
    local, inner_in, total, cross_in, outer, prefix, acc_sq, acc_in, stat_out, stat_in,
    kv_sem, in_sem,
    in_send, in_recv, cross_send, cross_recv, fwd_send, fwd_recv, stat_send, stat_recv,
):
    tokens, columns = q.shape
    tile = tokens // 2
    units = columns // PAIR
    half = units // 2
    chips = seq_size // 2
    me = lax.axis_index("seq")
    chip, core = me // 2, me % 2
    head = lax.axis_index("head")
    partner = chip * 2 + 1 - core

    def cols(unit):
        return pl.ds(pl.multiple_of(unit * PAIR, PAIR), PAIR)

    def own_unit(j):
        return core * half + j

    def other_unit(j):
        return (1 - core) * half + j

    def load(i, which):
        unit = lax.rem((1 - core) * half + i, units)
        source, target = ((k_hbm, k), (v_hbm, v))[which]
        return pltpu.make_async_copy(
            source.at[:, cols(unit)], target.at[:, cols(unit)], kv_sem.at[which, i]
        )

    def start_load(i, carry):
        for n in (i, half + i):
            load(n, 0).start()
            load(n, 1).start()
        return carry

    start_load(0, 0)
    load_q = pltpu.make_async_copy(q_hbm, q, in_sem.at[0])
    load_ct = pltpu.make_async_copy(ct_hbm, ct, in_sem.at[1])

    barrier = pltpu.get_barrier_semaphore()
    pl.semaphore_signal(barrier, inc=1, device_id={"seq": partner}, device_id_type=MESH)
    for d in range(1, chips):
        pl.semaphore_signal(
            barrier, inc=1, device_id={"seq": lax.rem(me + 2 * d, seq_size)}, device_id_type=MESH
        )
    for d in range(1, head_size):
        pl.semaphore_signal(
            barrier, inc=1, device_id={"head": lax.rem(head + d, head_size)}, device_id_type=MESH
        )
    pl.semaphore_wait(barrier, 1 + (chips - 1) + (head_size - 1))
    lax.fori_loop(1, half, start_load, 0)
    load_q.start()
    load_ct.start()

    def states(unit):
        return pl.ds(2 * unit, 2)

    def to_partner(way, i):
        unit = lax.rem((1 - core) * half + i, units)
        return pltpu.make_async_remote_copy(
            src_ref=local.at[way, states(unit)],
            dst_ref=inner_in.at[way, states(unit)],
            send_sem=in_send.at[way, i],
            recv_sem=in_recv.at[way, i],
            device_id={"seq": partner},
            device_id_type=MESH,
        )

    def across(way, d, j):
        step = 2 * d if way == 0 else -2 * d
        return pltpu.make_async_remote_copy(
            src_ref=total.at[way, states(j)],
            dst_ref=cross_in.at[way, d - 1, states(j)],
            send_sem=cross_send.at[way, d - 1, j],
            recv_sem=cross_recv.at[way, d - 1, j],
            device_id={"seq": lax.rem(me + step + seq_size, seq_size)},
            device_id_type=MESH,
        )

    def forward(way, j, unit):
        return pltpu.make_async_remote_copy(
            src_ref=outer.at[way, states(unit)],
            dst_ref=outer.at[way, states(unit)],
            send_sem=fwd_send.at[way, j],
            recv_sem=fwd_recv.at[way, j],
            device_id={"seq": partner},
            device_id_type=MESH,
        )

    def sends_to(way, d):
        return chip + d < chips if way == 0 else chip - d >= 0

    def takes_from(way, d):
        return chip - d >= 0 if way == 0 else chip + d < chips

    def takes_any(way):
        return chip > 0 if way == 0 else chip < chips - 1

    def gives_inner(way):
        return core == 0 if way == 0 else core == 1

    def send_states(way, make):
        def give_other(i):
            make(i, other_unit(i))
            to_partner(way, i).start()

        give_other(0)

        def step(j, carry):
            unit = own_unit(j)
            make(half + j, unit)

            @pl.when(gives_inner(way))
            def _():
                to_partner(way, half + j).start()

            @pl.when(j + 1 < half)
            def _():
                give_other(j + 1)

            to_partner(way, j).wait_recv()
            total[way, states(j)] = local[way, states(unit)] + inner_in[way, states(unit)]
            for d in range(1, chips):

                @pl.when(sends_to(way, d))
                def _():
                    across(way, d, j).start()

            return carry

        lax.fori_loop(0, half, step, 0)

    def take_states(way, use):
        def step(j, carry):
            unit = own_unit(j)

            @pl.when(takes_any(way))
            def _():
                outer[way, states(unit)] = jnp.zeros((2, HD, HD), F32)
                for d in range(1, chips):

                    @pl.when(takes_from(way, d))
                    def _():
                        across(way, d, j).wait_recv()
                        outer[way, states(unit)] += cross_in[way, d - 1, states(j)]

                forward(way, j, unit).start()

            @pl.when(jnp.logical_not(takes_any(way)))
            def _():
                outer[way, states(unit)] = jnp.zeros((2, HD, HD), F32)
                outer[way, states(other_unit(j))] = jnp.zeros((2, HD, HD), F32)

            use(unit, low_state(way, unit))

            @pl.when(takes_any(way))
            def _():
                forward(way, j, other_unit(j)).wait_recv()

            @pl.when(jnp.logical_not(gives_inner(way)))
            def _():
                to_partner(way, half + j).wait_recv()

            use(other_unit(j), low_state(way, other_unit(j)))
            return carry

        lax.fori_loop(0, half, step, 0)

    def low_state(way, unit):
        state = outer[way, states(unit)]
        state = jnp.where(gives_inner(way), state, state + inner_in[way, states(unit)])
        state = state.astype(BF16)
        return block_diagonal(state[0], state[1])

    def end_sends(way):
        def step(j, carry):
            to_partner(way, j).wait_send()

            @pl.when(gives_inner(way))
            def _():
                to_partner(way, half + j).wait_send()

            for d in range(1, chips):

                @pl.when(sends_to(way, d))
                def _():
                    across(way, d, j).wait_send()

            @pl.when(takes_any(way))
            def _():
                forward(way, j, own_unit(j)).wait_send()

            return carry

        lax.fori_loop(0, half, step, 0)

    def put_state(way, unit, both):
        local[way, 2 * unit] = both[:HD, :HD]
        local[way, 2 * unit + 1] = both[HD:, HD:]

    def make_kv(i, unit):
        load(i, 0).wait()
        load(i, 1).wait()
        put_state(0, unit, dot(k[:, cols(unit)], v[:, cols(unit)], 0, 0))

    send_states(0, make_kv)

    def causal(scores):
        row = lax.broadcasted_iota(jnp.int32, (tile, tile), 0)
        column = lax.broadcasted_iota(jnp.int32, (tile, tile), 1)
        return jnp.where(row >= column, scores, 0.0).astype(BF16)

    def three_tiles(rows, columns):
        left = dot(rows, columns[:tile], 1, 1)
        right = dot(rows[tile:], columns[tile:], 1, 1)
        return causal(left[:tile]), left[tile:].astype(BF16), causal(right)

    def times(tiles, values):
        t00, t10, t11 = tiles
        first = dot(jnp.concatenate([t00, t10], axis=0), values[:tile], 1, 0)
        return first[:tile], first[tile:] + dot(t11, values[tile:], 1, 0)

    def turned_times(tiles, values):
        t00, t10, t11 = tiles
        second = dot(jnp.concatenate([t10, t11], axis=1), values[tile:], 0, 0)
        return second[:tile] + dot(t00, values[:tile], 0, 0), second[tile:]

    acc_sq[...] = jnp.zeros_like(acc_sq)
    acc_in[...] = jnp.zeros_like(acc_in)
    load_q.wait()

    def own_scores(unit, carry):
        query, key, value = q[:, cols(unit)], k[:, cols(unit)], v[:, cols(unit)]
        for n in range(2):
            at = slice(n * HD, (n + 1) * HD)
            qh, kh, vh = query[:, at], key[:, at], value[:, at]
            tiles = three_tiles(qh, kh)
            for m in range(3):
                weights[2 * unit + n, m] = tiles[m]
            where = pl.ds(pl.multiple_of(unit * PAIR + n * HD, HD), HD)
            att[:tile, where], att[tile:, where] = times(tiles, vh)
        return carry

    lax.fori_loop(0, units, own_scores, 0, unroll=2)
    load_ct.wait()

    def add_prefix(unit, low):
        prefix[unit] = low
        attended = att[:, cols(unit)] + dot(q[:, cols(unit)], low, 1, 0)
        att[:, cols(unit)] = attended
        squared = attended * attended
        product = ct[:, cols(unit)].astype(F32) * gain_ref[:, cols(unit)] * attended
        acc_sq[...] += squared[:, :HD] + squared[:, HD:]
        acc_in[...] += product[:, :HD] + product[:, HD:]

    take_states(0, add_prefix)

    stat_out[0:1, :] = jnp.sum(acc_sq[...].T, axis=0, keepdims=True)
    stat_out[1:2, :] = jnp.sum(acc_in[...].T, axis=0, keepdims=True)
    stat_out[2:8, :] = jnp.zeros((6, tokens), F32)

    def stat_copy(d):
        return pltpu.make_async_remote_copy(
            src_ref=stat_out,
            dst_ref=stat_in.at[d - 1],
            send_sem=stat_send.at[d - 1],
            recv_sem=stat_recv.at[d - 1],
            device_id={"head": lax.rem(head + d, head_size)},
            device_id_type=MESH,
        )

    for d in range(1, head_size):
        stat_copy(d).start()
    sums = stat_out[...]
    for d in range(1, head_size):
        stat_copy(d).wait_recv()
        sums = sums + stat_in[d - 1]
    inverse = lax.rsqrt(sums[0:1] / FEAT + EPS)
    scale = sums[1:2] * inverse * inverse * inverse / FEAT
    acc_sq[...] = jnp.broadcast_to(inverse, (HD, tokens)).T
    acc_in[...] = jnp.broadcast_to(scale, (HD, tokens)).T

    def make_qg(i, unit):
        gain = gain_ref[:, cols(unit)]
        inv = jnp.concatenate([acc_sq[...]] * 2, axis=1)
        coef = jnp.concatenate([acc_in[...]] * 2, axis=1)
        attended = att[:, cols(unit)]
        scaled = ct[:, cols(unit)].astype(F32) * gain
        out_grad = (inv * scaled - attended * coef).astype(BF16)
        og[:, cols(unit)] = out_grad
        put_state(1, unit, dot(q[:, cols(unit)], out_grad, 0, 0))

    send_states(1, make_qg)

    part_k = att

    def own_grads(unit, carry):
        query, key, value = q[:, cols(unit)], k[:, cols(unit)], v[:, cols(unit)]
        grad = og[:, cols(unit)]
        inv = jnp.concatenate([acc_sq[...]] * 2, axis=1)
        lo[:, cols(unit)] = (att[:, cols(unit)] * inv * gain_ref[:, cols(unit)]).astype(BF16)
        from_prefix = dot(grad, prefix[unit], 1, 1)
        for n in range(2):
            at = slice(n * HD, (n + 1) * HD)
            qh, kh, vh, gh = query[:, at], key[:, at], value[:, at], grad[:, at]
            tiles = three_tiles(gh, vh)
            kept = [weights[2 * unit + n, m] for m in range(3)]
            where = pl.ds(pl.multiple_of(unit * PAIR + n * HD, HD), HD)
            upper, lower = times(tiles, kh)
            gq[:tile, where] = (from_prefix[:tile, at] + upper).astype(BF16)
            gq[tile:, where] = (from_prefix[tile:, at] + lower).astype(BF16)
            part_k[:tile, where], part_k[tile:, where] = turned_times(tiles, qh)
            part_v[:tile, where], part_v[tile:, where] = turned_times(kept, gh)
        return carry

    lax.fori_loop(0, units, own_grads, 0, unroll=2)

    def add_suffix(unit, low):
        at = cols(unit)
        gk[:, at] = (part_k[:, at] + dot(v[:, at], low, 1, 1)).astype(BF16)
        gv[:, at] = (part_v[:, at] + dot(k[:, at], low, 1, 0)).astype(BF16)

    take_states(1, add_suffix)

    end_sends(0)
    end_sends(1)
    for d in range(1, head_size):
        stat_copy(d).wait_send()


def write_out(*refs):
    sources, targets, sems = refs[:4], refs[4:8], refs[8]
    rows = sources[0].shape[0] // 4
    copies = [
        pltpu.make_async_copy(
            source.at[pl.ds(part * rows, rows)], target.at[pl.ds(part * rows, rows)], sems.at[n, part]
        )
        for part in range(4)
        for n, (source, target) in enumerate(zip(sources, targets))
    ]
    for copy in copies:
        copy.start()
    for copy in copies:
        copy.wait()


def per_device(seq_size, head_size, queries, key_vectors, value_vectors, norm_gain, cotangent):
    tokens, columns = queries.shape
    heads = columns // HD
    units = heads // 2
    half = units // 2
    chips = seq_size // 2
    dma = pltpu.SemaphoreType.DMA
    in_hbm = pl.BlockSpec(memory_space=pltpu.HBM)
    narrow = pltpu.VMEM((tokens, columns), BF16)
    wide = pltpu.VMEM((tokens, columns), F32)
    results = pl.pallas_call(
        functools.partial(kernel, seq_size, head_size),
        out_shape=(narrow,) * 4,
        in_specs=[in_hbm] * 3 + [pl.BlockSpec(memory_space=pltpu.VMEM), in_hbm],
        out_specs=(pl.BlockSpec(memory_space=pltpu.VMEM),) * 4,
        scratch_shapes=[narrow] * 4
        + [
            pltpu.VMEM((heads, 3, tokens // 2, tokens // 2), BF16),
            wide,
            narrow,
            wide,
            pltpu.VMEM((2, heads, HD, HD), F32),
            pltpu.VMEM((2, heads, HD, HD), F32),
            pltpu.VMEM((2, heads // 2, HD, HD), F32),
            pltpu.VMEM((2, max(chips - 1, 1), heads // 2, HD, HD), F32),
            pltpu.VMEM((2, heads, HD, HD), F32),
            pltpu.VMEM((units, PAIR, PAIR), BF16),
            pltpu.VMEM((tokens, HD), F32),
            pltpu.VMEM((tokens, HD), F32),
            pltpu.VMEM((8, tokens), F32),
            pltpu.VMEM((max(head_size - 1, 1), 8, tokens), F32),
            dma((2, units)),
            dma((2,)),
            dma((2, units)),
            dma((2, units)),
            dma((2, max(chips - 1, 1), half)),
            dma((2, max(chips - 1, 1), half)),
            dma((2, half)),
            dma((2, half)),
            dma((max(head_size - 1, 1),)),
            dma((max(head_size - 1, 1),)),
        ],
        compiler_params=pltpu.CompilerParams(
            collective_id=0, has_side_effects=True, vmem_limit_bytes=48 * 1024 * 1024
        ),
        cost_estimate=pl.CostEstimate(
            flops=12 * tokens * tokens * columns,
            bytes_accessed=16 * tokens * columns,
            transcendentals=tokens,
        ),
    )(queries, key_vectors, value_vectors, norm_gain.reshape(1, columns), cotangent)
    out = jax.ShapeDtypeStruct((tokens, columns), BF16)
    return pl.pallas_call(
        write_out,
        out_shape=(out,) * 4,
        in_specs=[pl.BlockSpec(memory_space=pltpu.VMEM)] * 4,
        compiler_params=pltpu.CompilerParams(vmem_limit_bytes=1024 * 1024),
        out_specs=(pl.BlockSpec(memory_space=pltpu.HBM),) * 4,
        scratch_shapes=[dma((4, 4))],
        cost_estimate=pl.CostEstimate(
            flops=0, bytes_accessed=8 * tokens * columns, transcendentals=0
        ),
    )(*results)


def solution(mesh):
    rows, features = P(("dp", "seq"), "head"), P("head")
    return jax.shard_map(
        functools.partial(per_device, mesh.shape["seq"], mesh.shape["head"]),
        mesh=mesh,
        in_specs=(rows, rows, rows, features, rows),
        out_specs=(rows,) * 4,
        check_vma=False,
    )
```
